32 devices in a mesh: seq: 8 (over y, x, core), ch: 4 (over z).
Axes of the slice: x: 2, y: 2, z: 4, core: 2. Of those that a mesh axis runs over, the one named last changes fastest.
Arguments:
- inputs: bfloat16 [2048, 4096], P('seq', 'ch'), may hold values from -6 to 6
- w_value: bfloat16 [4096, 4096], P(None, 'ch'), may hold values from -0.09375 to 0.09375
- gates: bfloat16 [2, 2048, 4096], P(None, 'seq', 'ch'), may hold values from -6 to 6
- decay_rate: float32 [16, 4096], P(None, 'ch'), may hold values from 0 to 0.125, as said below
- residue: float32 [16, 4096], P(None, 'ch'), may hold values from -5 to 5
- fir_taps: float32 [128, 4096], P(None, 'ch'), may hold values from -0.5 to 0.5
- skip_gain: float32 [4096], P('ch'), may hold values from -4 to 4
Outputs:
- mixed: bfloat16 [2048, 4096], P('seq', 'ch')
The draws below stay inside these ranges and needn't reach their ends.
Inputs may be any that keep to these rules, and one draw needn't show every extreme that they name: `decay_rate`: every rate is positive.
All inputs are finite; a program needn't handle non-finite values.
Results may differ from the reference program's by a relative error of at most 0.0049.
Values may be sent and summed in bfloat16 or wider, within the bound.
A program may use at most 384 MiB of HBM per device.

```python
import jax
import jax.numpy as jnp
from jax import lax

D = 4096
POLES = 16
TAPS = 128
TOKENS = 2048


def draw_decay_rate(key, part):
    first, second, third = jax.random.split(key, 3)
    slow_share = 0.5
    picker = jax.random.uniform(first, (POLES, D), jnp.float32)
    slow_rate = jnp.exp(jnp.log(0.05 / TOKENS) + jax.random.uniform(second, (POLES, D), jnp.float32) * jnp.log(30.0))
    fast_rate = jnp.exp(jnp.log(1.0 / 64.0) + jax.random.uniform(third, (POLES, D), jnp.float32) * jnp.log(8.0))
    return jnp.where(picker < slow_share, slow_rate, fast_rate).astype(jnp.float32)


def block_levels(own_key, extent, cuts, least, high):
    loudness, own = 1.0, jax.random.fold_in(own_key, 6)
    for position, shards_of in cuts:
        steps = jnp.exp(jax.random.uniform(jax.random.fold_in(own, position), (shards_of,), jnp.float32, least / len(cuts), high / len(cuts)))
        loudness = loudness * jnp.repeat(steps, extent[position] // shards_of).reshape([-1 if axis == position else 1 for axis in range(len(extent))])
    return loudness


def scatter_about(stream_key, dims, spread, bound, shards=(), held_as=jnp.bfloat16):
    array = jax.random.normal(stream_key, dims, jnp.float32) * spread
    if len(shards) > 0:
        array = block_levels(stream_key, dims, shards, -0.22, 0.18) * array
    return jnp.clip(array, min=-bound, max=bound).astype(held_as)


def setup_inputs(seed: int = 0) -> dict:
    keys = jax.random.split(jax.random.key(seed), 8)
    inputs = scatter_about(keys[0], (TOKENS, D), 1.0, 6.0, ((0, 8), (1, 4)))
    w_value = scatter_about(keys[1], (D, D), D ** -0.5, 0.09375, ((1, 4),))
    gates = scatter_about(keys[2], (2, TOKENS, D), 1.0, 6.0, ((1, 8), (2, 4)))
    decay_rate = draw_decay_rate(jax.random.fold_in(keys[7], 71), 0)
    residue = scatter_about(keys[4], (POLES, D), 1.0, 5.0, ((1, 4),), jnp.float32)
    fir_taps = scatter_about(keys[5], (TAPS, D), TAPS ** -0.5, 0.5, ((1, 4),), jnp.float32)
    skip_gain = scatter_about(keys[6], (D,), 1.0, 4.0, ((0, 4),), jnp.float32)
    return {"inputs": inputs, "w_value": w_value, "gates": gates, "decay_rate": decay_rate, "residue": residue, "fir_taps": fir_taps, "skip_gain": skip_gain}


def reference(inputs, w_value, gates, decay_rate, residue, fir_taps, skip_gain):
    projected = jnp.dot(inputs, w_value, preferred_element_type=jnp.float32)
    signal_low = (gates[1].astype(jnp.float32) * projected).astype(jnp.bfloat16)
    signal = lax.optimization_barrier(signal_low).astype(jnp.float32)
    modal_coef = residue * jnp.sqrt(-jnp.expm1(-2.0 * decay_rate))
    chan_block_size = min(256, D)
    fft_length = 2 * TOKENS

    def convolve_block(block_index):
        start = block_index * chan_block_size
        chan_block = lax.dynamic_slice_in_dim(signal, start, chan_block_size, 1)
        rates = lax.dynamic_slice_in_dim(decay_rate, start, chan_block_size, 1)
        coefs = lax.dynamic_slice_in_dim(modal_coef, start, chan_block_size, 1)
        heads = lax.dynamic_slice_in_dim(fir_taps, start, chan_block_size, 1)
        lag_times = jnp.arange(TOKENS).astype(signal.dtype)[:, None]
        filter_taps = jnp.zeros((TOKENS, chan_block_size), signal.dtype)
        for pole in range(POLES):
            filter_taps = filter_taps + coefs[pole] * jnp.exp(-rates[pole] * lag_times)
        filter_taps = filter_taps.at[:TAPS].add(heads)
        spectrum = jnp.fft.rfft(chan_block, n=fft_length, axis=0) * jnp.fft.rfft(filter_taps, n=fft_length, axis=0)
        return jnp.fft.irfft(spectrum, n=fft_length, axis=0)[:TOKENS].astype(signal.dtype)
    conv_blocks = lax.map(convolve_block, jnp.arange(D // chan_block_size).astype(jnp.int32))
    conv = jnp.transpose(conv_blocks, (1, 0, 2)).reshape(TOKENS, D)
    mixed = gates[0].astype(jnp.float32) * (conv + skip_gain * signal)
    return mixed.astype(jnp.bfloat16)
```

```python
import functools

import jax
import jax.numpy as jnp
from jax import lax
from jax.experimental import pallas as pl
from jax.experimental.pallas import tpu as pltpu
from jax.sharding import PartitionSpec as P

MESH = pl.DeviceIdType.MESH
SUB = 8
LANES = 128
TILE = 16
CHUNK = 64
f32 = jnp.float32
bf16 = jnp.bfloat16


def fused(seqs, chs, x_ref, w_ref, gates_ref, rate_ref, res_ref, fir_ref, skip_ref, out_ref,
          x_all, w_v, sig, x3, y3, f3, q3, c3, qc3, qr3, ends, tail_in, st_out, st_in, inc,
          acc, send_sem, recv_sem, w_sem, tail_sem, st_send_sem, st_recv_sem):
    rows, depth = x_ref.shape
    width = w_ref.shape[1]
    groups = width // LANES
    taps = fir_ref.shape[0]
    poles = rate_ref.shape[0]
    chunks = rows // CHUNK
    state_rows = poles * SUB
    s = lax.axis_index("seq")
    z = lax.axis_index("ch")

    def at_rows(start, size):
        return pl.ds(pl.multiple_of(start * SUB, SUB), size * SUB)

    barrier = pltpu.get_barrier_semaphore()

    def greet(other, carry):
        @pl.when(other != s)
        def _():
            pl.semaphore_signal(barrier, inc=1, device_id={"seq": other}, device_id_type=MESH)
        return carry

    lax.fori_loop(0, seqs, greet, 0)

    @pl.when(z > 0)
    def _():
        pl.semaphore_signal(barrier, inc=1, device_id={"ch": z - 1}, device_id_type=MESH)

    @pl.when(z < chs - 1)
    def _():
        pl.semaphore_signal(barrier, inc=1, device_id={"ch": z + 1}, device_id_type=MESH)

    def w_copy(origin):
        block = pl.ds(pl.multiple_of(origin * depth, depth), depth)
        return pltpu.make_async_copy(w_ref.at[block, :], w_v.at[block, :], w_sem.at[origin])

    w_copy(z).start()
    for d in range(1, chs):
        @pl.when(z - d >= 0)
        def _():
            w_copy(z - d).start()

        @pl.when(z + d <= chs - 1)
        def _():
            w_copy(z + d).start()

    neighbours = jnp.minimum(z, 1) + jnp.minimum(chs - 1 - z, 1)
    pl.semaphore_wait(barrier, seqs - 1 + neighbours)

    def chunk_rows(c):
        return pl.ds(pl.multiple_of(c * CHUNK, CHUNK), CHUNK)

    def hop(way, d, c):
        step = 1 - 2 * way
        origin = z - step * d
        src = x_ref.at[chunk_rows(c), :] if d == 0 else x_all.at[origin, chunk_rows(c), :]
        return pltpu.make_async_remote_copy(
            src_ref=src, dst_ref=x_all.at[origin, chunk_rows(c), :],
            send_sem=send_sem.at[way, d, c], recv_sem=recv_sem.at[way, d + 1, c],
            device_id={"ch": z + step}, device_id_type=MESH)

    def landed(way, d, c):
        step = 1 - 2 * way
        origin = z - step * d
        place = x_all.at[origin, chunk_rows(c), :]
        return pltpu.make_async_remote_copy(
            src_ref=place, dst_ref=place,
            send_sem=send_sem.at[way, d, c], recv_sem=recv_sem.at[way, d, c],
            device_id={"ch": z - step}, device_id_type=MESH)

    def comes(way, d):
        return z - d >= 0 if way == 0 else z + d <= chs - 1

    def goes(way):
        return z < chs - 1 if way == 0 else z > 0

    def send_own(c):
        for way in range(2):
            @pl.when(goes(way))
            def _():
                hop(way, 0, c).start()

    send_own(chunks - 1)
    send_own(chunks - 2)

    def spread(dst, first, value, count):
        for j in range(groups):
            dst[pl.ds(first * SUB + j, count, stride=SUB), :] = value[:, j * LANES:(j + 1) * LANES]

    rate = rate_ref[...]
    decay = jnp.exp(-rate)
    spread(q3, 0, decay, poles)
    spread(qc3, 0, jnp.exp(-rate * CHUNK), poles)
    spread(qr3, 0, jnp.exp(-rate * rows), poles)
    two = jnp.exp(-2.0 * rate)
    spread(c3, 0, res_ref[...] * jnp.sqrt(jnp.tanh(rate) * (1.0 + two)), poles)
    f3[0:TILE * SUB, :] = jnp.zeros((TILE * SUB, LANES), f32)
    f3[(TILE + taps) * SUB:, :] = jnp.zeros((TILE * SUB, LANES), f32)
    spread(f3, TILE, fir_ref[...], taps)
    y3[...] = jnp.zeros_like(y3)
    inc[...] = jnp.zeros_like(inc)

    def multiply(lhs, origin, first):
        for n in range(0, width, 512):
            cols = slice(n, n + 512)
            block = pl.ds(pl.multiple_of(origin * depth, depth), depth)
            product = jnp.dot(lhs, w_v[block, cols], preferred_element_type=f32)
            if first:
                acc[:, cols] = product
            else:
                acc[:, cols] += product

    def fir_tiles(first, last, low, high):
        def tile(t, carry):
            y = tuple(y3[at_rows(t * TILE + i, 1), :] for i in range(TILE))

            def step(b, y):
                xs = x3[at_rows(taps + 8 * b, 8), :]
                fs = f3[at_rows(TILE + t * TILE - 8 * b - 7, 7 + TILE), :]
                y = list(y)
                for k in range(8):
                    xk = xs[k * SUB:(k + 1) * SUB]
                    for i in range(TILE):
                        m = i - k + 7
                        y[i] = y[i] + fs[m * SUB:(m + 1) * SUB] * xk
                return tuple(y)

            y = lax.fori_loop(jnp.maximum(low, 2 * t - taps // 8),
                              jnp.minimum(high, 2 * t + 2), step, y)
            for i in range(TILE):
                y3[at_rows(t * TILE + i, 1), :] = y[i]
            return carry

        lax.fori_loop(first, last, tile, 0)

    per = CHUNK // TILE
    reach = per + taps // TILE
    tiles = rows // TILE

    def fir_chunk(c, half):
        first = c * per + half * (reach // 2)
        last = jnp.minimum(tiles, first + reach // 2)
        fir_tiles(first, last, c * (CHUNK // 8), (c + 1) * (CHUNK // 8))

    def tree(terms):
        while len(terms) > 1:
            terms = [a + b for a, b in zip(terms[::2], terms[1::2])]
        return terms[0]

    def modal_chunk(c):
        q = [q3[p * SUB:(p + 1) * SUB, :] for p in range(poles)]
        coef = [c3[p * SUB:(p + 1) * SUB, :] for p in range(poles)]

        def step(i, state):
            at = c * CHUNK + i
            x = x3[at_rows(taps + at, 1), :]
            state = tuple(q[p] * state[p] + coef[p] * x for p in range(poles))
            y3[at_rows(at, 1), :] += tree(list(state))
            return state

        zero = jnp.zeros((SUB, LANES), f32)
        state = lax.fori_loop(0, CHUNK, step, (zero,) * poles)
        ends[c] = jnp.concatenate(state, axis=0)

    def tail_copy():
        return pltpu.make_async_remote_copy(
            src_ref=sig.at[pl.ds(rows - taps, taps), :], dst_ref=tail_in,
            send_sem=tail_sem.at[0], recv_sem=tail_sem.at[1],
            device_id={"seq": s + 1}, device_id_type=MESH)

    def fir_tail():
        @pl.when(s > 0)
        def _():
            pltpu.make_async_remote_copy(
                src_ref=tail_in, dst_ref=tail_in,
                send_sem=tail_sem.at[0], recv_sem=tail_sem.at[1],
                device_id={"seq": s - 1}, device_id_type=MESH).wait_recv()
            spread(x3, 0, tail_in[...].astype(f32), taps)
            fir_tiles(0, taps // TILE, -(taps // 8), 0)

    w_copy(z).wait()

    def chunk_step(i, carry):
        c = chunks - 1 - i

        @pl.when(i + 2 < chunks)
        def _():
            send_own(c - 2)

        multiply(x_ref[chunk_rows(c), :], z, True)
        for d in range(1, chs):
            for way in range(2):
                step = 1 - 2 * way

                @pl.when(comes(way, d))
                def _():
                    landed(way, d, c).wait_recv()

                    if d < chs - 1:
                        @pl.when(goes(way))
                        def _():
                            hop(way, d, c).start()

            for way in range(2):
                step = 1 - 2 * way

                @pl.when(comes(way, d))
                def _():
                    origin = z - step * d

                    @pl.when(i == 0)
                    def _():
                        w_copy(origin).wait()
                    multiply(x_all[origin, chunk_rows(c), :], origin, False)

            @pl.when(i > 0)
            def _():
                if d == 1:
                    modal_chunk(c + 1)
                if d == min(2, chs - 1):
                    fir_chunk(c + 1, 0)
                if d == min(3, chs - 1):
                    fir_chunk(c + 1, 1)

            if d == min(2, chs - 1):
                @pl.when(i == chunks - 1)
                def _():
                    fir_tail()

        low = (gates_ref[1, chunk_rows(c), :].astype(f32) * acc[...]).astype(bf16)
        sig[chunk_rows(c), :] = low
        spread(x3, taps + c * CHUNK, low.astype(f32), CHUNK)

        @pl.when((i == taps // CHUNK - 1) & (s < seqs - 1))
        def _():
            tail_copy().start()
        return carry

    lax.fori_loop(0, chunks, chunk_step, 0)

    modal_chunk(0)
    total = ends[0]
    for c in range(1, chunks):
        total = qc3[...] * total + ends[c]
    st_out[...] = total

    def state_copy(other):
        return pltpu.make_async_remote_copy(
            src_ref=st_out, dst_ref=st_in.at[s],
            send_sem=st_send_sem.at[other], recv_sem=st_recv_sem.at[s],
            device_id={"seq": other}, device_id_type=MESH)

    def start_state(other, carry):
        state_copy(other).start()
        return carry

    lax.fori_loop(s + 1, seqs, start_state, 0)
    fir_chunk(0, 0)
    fir_chunk(0, 1)

    def take_state(other, carry):
        pltpu.make_async_remote_copy(
            src_ref=st_out, dst_ref=st_in.at[other],
            send_sem=st_send_sem.at[other], recv_sem=st_recv_sem.at[other],
            device_id={"seq": other}, device_id_type=MESH).wait_recv()
        inc[...] = qr3[...] * inc[...] + st_in[other]
        return carry

    lax.fori_loop(0, s, take_state, 0)

    q = [q3[p * SUB:(p + 1) * SUB, :] for p in range(poles)]
    for c in range(chunks):
        def step(i, state):
            at = c * CHUNK + i
            state = tuple(q[p] * state[p] for p in range(poles))
            y3[at_rows(at, 1), :] += tree(list(state))
            return state

        state = tuple(inc[p * SUB:(p + 1) * SUB, :] for p in range(poles))
        state = lax.fori_loop(0, CHUNK, step, state)
        inc[...] = jnp.concatenate(state, axis=0) + ends[c]
        part = slice(c * CHUNK, (c + 1) * CHUNK)
        for j in range(groups):
            cols = slice(j * LANES, (j + 1) * LANES)
            conv = y3[pl.ds(c * CHUNK * SUB + j, CHUNK, stride=SUB), :]
            direct = skip_ref[:, cols] * sig[part, cols].astype(f32)
            out_ref[part, cols] = (gates_ref[0, part, cols].astype(f32) * (conv + direct)).astype(bf16)

    def end_state(other, carry):
        state_copy(other).wait_send()
        return carry

    lax.fori_loop(s + 1, seqs, end_state, 0)

    @pl.when(s < seqs - 1)
    def _():
        tail_copy().wait_send()

    def end_chunk(c, carry):
        for way in range(2):
            for d in range(chs - 1):
                @pl.when(comes(way, d) & goes(way))
                def _():
                    hop(way, d, c).wait_send()
        return carry

    lax.fori_loop(0, chunks, end_chunk, 0)


def on_device(inputs, w_value, gates, decay_rate, residue, fir_taps, skip_gain):
    seqs, chs = lax.axis_size("seq"), lax.axis_size("ch")
    rows, depth = inputs.shape
    width = w_value.shape[1]
    taps = fir_taps.shape[0]
    poles = decay_rate.shape[0]
    chunks = rows // CHUNK
    state = (poles * SUB, LANES)
    vmem = pl.BlockSpec(memory_space=pltpu.VMEM)
    return pl.pallas_call(
        functools.partial(fused, seqs, chs),
        out_shape=jax.ShapeDtypeStruct((rows, width), bf16),
        in_specs=[vmem, pl.BlockSpec(memory_space=pl.ANY)] + [vmem] * 5,
        out_specs=vmem,
        scratch_shapes=[
            pltpu.VMEM((chs, rows, depth), bf16),
            pltpu.VMEM(w_value.shape, bf16),
            pltpu.VMEM((rows, width), bf16),
            pltpu.VMEM(((taps + rows) * SUB, LANES), f32),
            pltpu.VMEM((rows * SUB, LANES), f32),
            pltpu.VMEM(((taps + 2 * TILE) * SUB, LANES), f32),
            pltpu.VMEM(state, f32),
            pltpu.VMEM(state, f32),
            pltpu.VMEM(state, f32),
            pltpu.VMEM(state, f32),
            pltpu.VMEM((chunks,) + state, f32),
            pltpu.VMEM((taps, width), bf16),
            pltpu.VMEM(state, f32),
            pltpu.VMEM((seqs,) + state, f32),
            pltpu.VMEM(state, f32),
            pltpu.VMEM((CHUNK, width), f32),
            pltpu.SemaphoreType.DMA((2, chs, chunks)),
            pltpu.SemaphoreType.DMA((2, chs, chunks)),
            pltpu.SemaphoreType.DMA((chs,)),
            pltpu.SemaphoreType.DMA((2,)),
            pltpu.SemaphoreType.DMA((seqs,)),
            pltpu.SemaphoreType.DMA((seqs,)),
        ],
        compiler_params=pltpu.CompilerParams(
            collective_id=0, has_side_effects=True, vmem_limit_bytes=48 * 2**20),
        cost_estimate=pl.CostEstimate(
            flops=2 * rows * depth * chs * width, bytes_accessed=2 * depth * chs * width, transcendentals=0),
    )(inputs, w_value, gates, decay_rate, residue, fir_taps, skip_gain.reshape(1, width))


def solution(mesh):
    in_specs = (
        P("seq", "ch"),
        P(None, "ch"),
        P(None, "seq", "ch"),
        P(None, "ch"),
        P(None, "ch"),
        P(None, "ch"),
        P("ch"),
    )
    out_specs = P("seq", "ch")
    return jax.shard_map(
        on_device, mesh=mesh, in_specs=in_specs, out_specs=out_specs, check_vma=False
    )
```

```python
import functools

import jax
import jax.numpy as jnp
from jax import lax
from jax.experimental import pallas as pl
from jax.experimental.pallas import tpu as pltpu
from jax.sharding import PartitionSpec as P

MESH = pl.DeviceIdType.MESH
SUB = 8
LANES = 128
TILE = 16
CHUNK = 64
f32 = jnp.float32
bf16 = jnp.bfloat16


def fused(seqs, chs, x_ref, w_ref, gates_hbm, rate_hbm, res_hbm, fir_hbm, skip_hbm, out_ref,
          gates_ref, rate_ref, res_ref, fir_ref, skip_ref, x_all, w_v, sig, x3, y3, f3, q3, c3, qc3, qr3, ends, tail_in, st_out, st_in, inc,
          acc, send_sem, recv_sem, w_sem, load_sem, tail_sem, st_send_sem, st_recv_sem):
    rows, depth = x_ref.shape
    width = w_ref.shape[1]
    groups = width // LANES
    taps = fir_ref.shape[0]
    poles = rate_ref.shape[0]
    chunks = rows // CHUNK
    state_rows = poles * SUB
    s = lax.axis_index("seq")
    z = lax.axis_index("ch")

    def at_rows(start, size):
        return pl.ds(pl.multiple_of(start * SUB, SUB), size * SUB)

    barrier = pltpu.get_barrier_semaphore()

    def greet(other, carry):
        @pl.when(other != s)
        def _():
            pl.semaphore_signal(barrier, inc=1, device_id={"seq": other}, device_id_type=MESH)
        return carry

    lax.fori_loop(0, seqs, greet, 0)

    @pl.when(z > 0)
    def _():
        pl.semaphore_signal(barrier, inc=1, device_id={"ch": z - 1}, device_id_type=MESH)

    @pl.when(z < chs - 1)
    def _():
        pl.semaphore_signal(barrier, inc=1, device_id={"ch": z + 1}, device_id_type=MESH)

    def w_copy(origin):
        block = pl.ds(pl.multiple_of(origin * depth, depth), depth)
        return pltpu.make_async_copy(w_ref.at[block, :], w_v.at[block, :], w_sem.at[origin])

    pairs = ((rate_hbm, rate_ref), (res_hbm, res_ref), (fir_hbm, fir_ref), (skip_hbm, skip_ref),
             (x_ref, x_all.at[z]), (gates_hbm, gates_ref))
    loads = [pltpu.make_async_copy(src, dst, load_sem.at[n]) for n, (src, dst) in enumerate(pairs)]
    for load in loads:
        load.start()
    w_copy(z).start()
    for d in range(1, chs):
        @pl.when(z - d >= 0)
        def _():
            w_copy(z - d).start()

        @pl.when(z + d <= chs - 1)
        def _():
            w_copy(z + d).start()

    neighbours = jnp.minimum(z, 1) + jnp.minimum(chs - 1 - z, 1)
    pl.semaphore_wait(barrier, seqs - 1 + neighbours)

    def chunk_rows(c):
        return pl.ds(pl.multiple_of(c * CHUNK, CHUNK), CHUNK)

    def hop(way, d, c):
        step = 1 - 2 * way
        origin = z - step * d
        src = x_ref.at[chunk_rows(c), :] if d == 0 else x_all.at[origin, chunk_rows(c), :]
        return pltpu.make_async_remote_copy(
            src_ref=src, dst_ref=x_all.at[origin, chunk_rows(c), :],
            send_sem=send_sem.at[way, d, c], recv_sem=recv_sem.at[way, d + 1, c],
            device_id={"ch": z + step}, device_id_type=MESH)

    def landed(way, d, c):
        step = 1 - 2 * way
        origin = z - step * d
        place = x_all.at[origin, chunk_rows(c), :]
        return pltpu.make_async_remote_copy(
            src_ref=place, dst_ref=place,
            send_sem=send_sem.at[way, d, c], recv_sem=recv_sem.at[way, d, c],
            device_id={"ch": z - step}, device_id_type=MESH)

    def comes(way, d):
        return z - d >= 0 if way == 0 else z + d <= chs - 1

    def goes(way):
        return z < chs - 1 if way == 0 else z > 0

    def send_own(c):
        for way in range(2):
            @pl.when(goes(way))
            def _():
                hop(way, 0, c).start()

    send_own(chunks - 1)
    send_own(chunks - 2)

    def spread(dst, first, value, count):
        for j in range(groups):
            dst[pl.ds(first * SUB + j, count, stride=SUB), :] = value[:, j * LANES:(j + 1) * LANES]

    for load in loads[:4]:
        load.wait()
    rate = rate_ref[...]
    decay = jnp.exp(-rate)
    spread(q3, 0, decay, poles)
    spread(qc3, 0, jnp.exp(-rate * CHUNK), poles)
    spread(qr3, 0, jnp.exp(-rate * rows), poles)
    two = jnp.exp(-2.0 * rate)
    spread(c3, 0, res_ref[...] * jnp.sqrt(jnp.tanh(rate) * (1.0 + two)), poles)
    f3[0:TILE * SUB, :] = jnp.zeros((TILE * SUB, LANES), f32)
    f3[(TILE + taps) * SUB:, :] = jnp.zeros((TILE * SUB, LANES), f32)
    spread(f3, TILE, fir_ref[...], taps)
    y3[...] = jnp.zeros_like(y3)
    inc[...] = jnp.zeros_like(inc)

    def multiply(lhs, origin, first):
        for n in range(0, width, 512):
            cols = slice(n, n + 512)
            block = pl.ds(pl.multiple_of(origin * depth, depth), depth)
            product = jnp.dot(lhs, w_v[block, cols], preferred_element_type=f32)
            if first:
                acc[:, cols] = product
            else:
                acc[:, cols] += product

    def fir_tiles(first, last, low, high):
        def tile(t, carry):
            y = tuple(y3[at_rows(t * TILE + i, 1), :] for i in range(TILE))

            def step(b, y):
                xs = x3[at_rows(taps + 8 * b, 8), :]
                fs = f3[at_rows(TILE + t * TILE - 8 * b - 7, 7 + TILE), :]
                y = list(y)
                for k in range(8):
                    xk = xs[k * SUB:(k + 1) * SUB]
                    for i in range(TILE):
                        m = i - k + 7
                        y[i] = y[i] + fs[m * SUB:(m + 1) * SUB] * xk
                return tuple(y)

            y = lax.fori_loop(jnp.maximum(low, 2 * t - taps // 8),
                              jnp.minimum(high, 2 * t + 2), step, y)
            for i in range(TILE):
                y3[at_rows(t * TILE + i, 1), :] = y[i]
            return carry

        lax.fori_loop(first, last, tile, 0)

    per = CHUNK // TILE
    reach = per + taps // TILE
    tiles = rows // TILE

    def fir_chunk(c, half):
        first = c * per + half * (reach // 2)
        last = jnp.minimum(tiles, first + reach // 2)
        fir_tiles(first, last, c * (CHUNK // 8), (c + 1) * (CHUNK // 8))

    def tree(terms):
        while len(terms) > 1:
            terms = [a + b for a, b in zip(terms[::2], terms[1::2])]
        return terms[0]

    def modal_chunk(c):
        q = [q3[p * SUB:(p + 1) * SUB, :] for p in range(poles)]
        coef = [c3[p * SUB:(p + 1) * SUB, :] for p in range(poles)]

        def step(i, state):
            at = c * CHUNK + i
            x = x3[at_rows(taps + at, 1), :]
            state = tuple(q[p] * state[p] + coef[p] * x for p in range(poles))
            y3[at_rows(at, 1), :] += tree(list(state))
            return state

        zero = jnp.zeros((SUB, LANES), f32)
        state = lax.fori_loop(0, CHUNK, step, (zero,) * poles)
        ends[c] = jnp.concatenate(state, axis=0)

    def tail_copy():
        return pltpu.make_async_remote_copy(
            src_ref=sig.at[pl.ds(rows - taps, taps), :], dst_ref=tail_in,
            send_sem=tail_sem.at[0], recv_sem=tail_sem.at[1],
            device_id={"seq": s + 1}, device_id_type=MESH)

    def fir_tail():
        @pl.when(s > 0)
        def _():
            pltpu.make_async_remote_copy(
                src_ref=tail_in, dst_ref=tail_in,
                send_sem=tail_sem.at[0], recv_sem=tail_sem.at[1],
                device_id={"seq": s - 1}, device_id_type=MESH).wait_recv()
            spread(x3, 0, tail_in[...].astype(f32), taps)
            fir_tiles(0, taps // TILE, -(taps // 8), 0)

    for load in loads[4:]:
        load.wait()
    w_copy(z).wait()

    def chunk_step(i, carry):
        c = chunks - 1 - i

        @pl.when(i + 2 < chunks)
        def _():
            send_own(c - 2)

        multiply(x_all[z, chunk_rows(c), :], z, True)
        for d in range(1, chs):
            for way in range(2):
                step = 1 - 2 * way

                @pl.when(comes(way, d))
                def _():
                    landed(way, d, c).wait_recv()

                    if d < chs - 1:
                        @pl.when(goes(way))
                        def _():
                            hop(way, d, c).start()

            for way in range(2):
                step = 1 - 2 * way

                @pl.when(comes(way, d))
                def _():
                    origin = z - step * d

                    @pl.when(i == 0)
                    def _():
                        w_copy(origin).wait()
                    multiply(x_all[origin, chunk_rows(c), :], origin, False)

            @pl.when(i > 0)
            def _():
                if d == 1:
                    modal_chunk(c + 1)
                if d == min(2, chs - 1):
                    fir_chunk(c + 1, 0)
                if d == min(3, chs - 1):
                    fir_chunk(c + 1, 1)

            if d == min(2, chs - 1):
                @pl.when(i == chunks - 1)
                def _():
                    fir_tail()

        low = (gates_ref[1, chunk_rows(c), :].astype(f32) * acc[...]).astype(bf16)
        sig[chunk_rows(c), :] = low
        spread(x3, taps + c * CHUNK, low.astype(f32), CHUNK)

        @pl.when((i == taps // CHUNK - 1) & (s < seqs - 1))
        def _():
            tail_copy().start()
        return carry

    lax.fori_loop(0, chunks, chunk_step, 0)

    modal_chunk(0)
    total = ends[0]
    for c in range(1, chunks):
        total = qc3[...] * total + ends[c]
    st_out[...] = total

    def state_copy(other):
        return pltpu.make_async_remote_copy(
            src_ref=st_out, dst_ref=st_in.at[s],
            send_sem=st_send_sem.at[other], recv_sem=st_recv_sem.at[s],
            device_id={"seq": other}, device_id_type=MESH)

    def start_state(other, carry):
        state_copy(other).start()
        return carry

    lax.fori_loop(s + 1, seqs, start_state, 0)
    fir_chunk(0, 0)
    fir_chunk(0, 1)

    def take_state(other, carry):
        pltpu.make_async_remote_copy(
            src_ref=st_out, dst_ref=st_in.at[other],
            send_sem=st_send_sem.at[other], recv_sem=st_recv_sem.at[other],
            device_id={"seq": other}, device_id_type=MESH).wait_recv()
        inc[...] = qr3[...] * inc[...] + st_in[other]
        return carry

    lax.fori_loop(0, s, take_state, 0)

    q = [q3[p * SUB:(p + 1) * SUB, :] for p in range(poles)]
    for c in range(chunks):
        def step(i, state):
            at = c * CHUNK + i
            state = tuple(q[p] * state[p] for p in range(poles))
            y3[at_rows(at, 1), :] += tree(list(state))
            return state

        state = tuple(inc[p * SUB:(p + 1) * SUB, :] for p in range(poles))
        state = lax.fori_loop(0, CHUNK, step, state)
        inc[...] = jnp.concatenate(state, axis=0) + ends[c]
        part = slice(c * CHUNK, (c + 1) * CHUNK)
        for j in range(groups):
            cols = slice(j * LANES, (j + 1) * LANES)
            conv = y3[pl.ds(c * CHUNK * SUB + j, CHUNK, stride=SUB), :]
            direct = skip_ref[:, cols] * sig[part, cols].astype(f32)
            out_ref[part, cols] = (gates_ref[0, part, cols].astype(f32) * (conv + direct)).astype(bf16)

    def end_state(other, carry):
        state_copy(other).wait_send()
        return carry

    lax.fori_loop(s + 1, seqs, end_state, 0)

    @pl.when(s < seqs - 1)
    def _():
        tail_copy().wait_send()

    def end_chunk(c, carry):
        for way in range(2):
            for d in range(chs - 1):
                @pl.when(comes(way, d) & goes(way))
                def _():
                    hop(way, d, c).wait_send()
        return carry

    lax.fori_loop(0, chunks, end_chunk, 0)


def on_device(inputs, w_value, gates, decay_rate, residue, fir_taps, skip_gain):
    seqs, chs = lax.axis_size("seq"), lax.axis_size("ch")
    rows, depth = inputs.shape
    width = w_value.shape[1]
    taps = fir_taps.shape[0]
    poles = decay_rate.shape[0]
    chunks = rows // CHUNK
    state = (poles * SUB, LANES)
    vmem = pl.BlockSpec(memory_space=pltpu.VMEM)
    return pl.pallas_call(
        functools.partial(fused, seqs, chs),
        out_shape=jax.ShapeDtypeStruct((rows, width), bf16),
        in_specs=[pl.BlockSpec(memory_space=pltpu.HBM)] * 7,
        out_specs=vmem,
        scratch_shapes=[
            pltpu.VMEM(gates.shape, bf16),
            pltpu.VMEM(decay_rate.shape, f32),
            pltpu.VMEM(residue.shape, f32),
            pltpu.VMEM(fir_taps.shape, f32),
            pltpu.VMEM((1, width), f32),
            pltpu.VMEM((chs, rows, depth), bf16),
            pltpu.VMEM(w_value.shape, bf16),
            pltpu.VMEM((rows, width), bf16),
            pltpu.VMEM(((taps + rows) * SUB, LANES), f32),
            pltpu.VMEM((rows * SUB, LANES), f32),
            pltpu.VMEM(((taps + 2 * TILE) * SUB, LANES), f32),
            pltpu.VMEM(state, f32),
            pltpu.VMEM(state, f32),
            pltpu.VMEM(state, f32),
            pltpu.VMEM(state, f32),
            pltpu.VMEM((chunks,) + state, f32),
            pltpu.VMEM((taps, width), bf16),
            pltpu.VMEM(state, f32),
            pltpu.VMEM((seqs,) + state, f32),
            pltpu.VMEM(state, f32),
            pltpu.VMEM((CHUNK, width), f32),
            pltpu.SemaphoreType.DMA((2, chs, chunks)),
            pltpu.SemaphoreType.DMA((2, chs, chunks)),
            pltpu.SemaphoreType.DMA((chs,)),
            pltpu.SemaphoreType.DMA((6,)),
            pltpu.SemaphoreType.DMA((2,)),
            pltpu.SemaphoreType.DMA((seqs,)),
            pltpu.SemaphoreType.DMA((seqs,)),
        ],
        compiler_params=pltpu.CompilerParams(
            collective_id=0, has_side_effects=True, vmem_limit_bytes=48 * 2**20),
        cost_estimate=pl.CostEstimate(
            flops=2 * rows * depth * chs * width, bytes_accessed=2 * depth * chs * width, transcendentals=0),
    )(inputs, w_value, gates, decay_rate, residue, fir_taps, skip_gain.reshape(1, width))


def solution(mesh):
    in_specs = (
        P("seq", "ch"),
        P(None, "ch"),
        P(None, "seq", "ch"),
        P(None, "ch"),
        P(None, "ch"),
        P(None, "ch"),
        P("ch"),
    )
    out_specs = P("seq", "ch")
    return jax.shard_map(
        on_device, mesh=mesh, in_specs=in_specs, out_specs=out_specs, check_vma=False
    )
```

```python
import functools

import jax
import jax.numpy as jnp
from jax import lax
from jax.experimental import pallas as pl
from jax.experimental.pallas import tpu as pltpu
from jax.sharding import PartitionSpec as P

MESH = pl.DeviceIdType.MESH
SUB = 8
LANES = 128
TILE = 16
CHUNK = 64
f32 = jnp.float32
bf16 = jnp.bfloat16


def fused(seqs, chs, x_ref, w_ref, gates_hbm, rate_hbm, res_hbm, fir_hbm, skip_hbm, out_ref,
          gates_ref, rate_ref, res_ref, fir_ref, skip_ref, x_all, w_v, sig, x3, y3, f3, q3, c3, qc3, qr3, ends, tail_in, st_out, st_mate, st_in, inc, out_v,
          acc, send_sem, recv_sem, w_sem, load_sem, tail_sem, mate_sem, st_send_sem, st_recv_sem, out_sem):
    rows, depth = x_ref.shape
    width = w_ref.shape[1]
    groups = width // LANES
    taps = fir_ref.shape[0]
    poles = rate_ref.shape[0]
    chunks = rows // CHUNK
    state_rows = poles * SUB
    s = lax.axis_index("seq")
    z = lax.axis_index("ch")

    def at_rows(start, size):
        return pl.ds(pl.multiple_of(start * SUB, SUB), size * SUB)

    barrier = pltpu.get_barrier_semaphore()

    def greet(other, carry):
        same = (other - s) * (other - s)
        @pl.when((same > 0) & ((lax.rem(same, 2) == 0) | (same == 1)))
        def _():
            pl.semaphore_signal(barrier, inc=1, device_id={"seq": other}, device_id_type=MESH)
        return carry

    lax.fori_loop(0, seqs, greet, 0)

    @pl.when(z > 0)
    def _():
        pl.semaphore_signal(barrier, inc=1, device_id={"ch": z - 1}, device_id_type=MESH)

    @pl.when(z < chs - 1)
    def _():
        pl.semaphore_signal(barrier, inc=1, device_id={"ch": z + 1}, device_id_type=MESH)

    def w_copy(origin):
        block = pl.ds(pl.multiple_of(origin * depth, depth), depth)
        return pltpu.make_async_copy(w_ref.at[block, :], w_v.at[block, :], w_sem.at[origin])

    pairs = ((rate_hbm, rate_ref), (res_hbm, res_ref), (fir_hbm, fir_ref), (skip_hbm, skip_ref),
             (x_ref, x_all.at[z]), (gates_hbm, gates_ref))
    loads = [pltpu.make_async_copy(src, dst, load_sem.at[n]) for n, (src, dst) in enumerate(pairs)]
    for load in loads:
        load.start()
    w_copy(z).start()
    for d in range(1, chs):
        @pl.when(z - d >= 0)
        def _():
            w_copy(z - d).start()

        @pl.when(z + d <= chs - 1)
        def _():
            w_copy(z + d).start()

    neighbours = jnp.minimum(z, 1) + jnp.minimum(chs - 1 - z, 1)
    beside = jnp.minimum(s, 1) + jnp.minimum(seqs - 1 - s, 1)
    pl.semaphore_wait(barrier, seqs // 2 - 1 + beside + neighbours)

    def chunk_rows(c):
        return pl.ds(pl.multiple_of(c * CHUNK, CHUNK), CHUNK)

    def hop(way, d, c):
        step = 1 - 2 * way
        origin = z - step * d
        src = x_ref.at[chunk_rows(c), :] if d == 0 else x_all.at[origin, chunk_rows(c), :]
        return pltpu.make_async_remote_copy(
            src_ref=src, dst_ref=x_all.at[origin, chunk_rows(c), :],
            send_sem=send_sem.at[way, d, c], recv_sem=recv_sem.at[way, d + 1, c],
            device_id={"ch": z + step}, device_id_type=MESH)

    def landed(way, d, c):
        step = 1 - 2 * way
        origin = z - step * d
        place = x_all.at[origin, chunk_rows(c), :]
        return pltpu.make_async_remote_copy(
            src_ref=place, dst_ref=place,
            send_sem=send_sem.at[way, d, c], recv_sem=recv_sem.at[way, d, c],
            device_id={"ch": z - step}, device_id_type=MESH)

    def comes(way, d):
        return z - d >= 0 if way == 0 else z + d <= chs - 1

    def goes(way):
        return z < chs - 1 if way == 0 else z > 0

    def send_own(c):
        for way in range(2):
            @pl.when(goes(way))
            def _():
                hop(way, 0, c).start()

    send_own(chunks - 1)

    def spread(dst, first, value, count):
        for j in range(groups):
            dst[pl.ds(first * SUB + j, count, stride=SUB), :] = value[:, j * LANES:(j + 1) * LANES]

    for load in loads[:4]:
        load.wait()
    rate = rate_ref[...]
    decay = jnp.exp(-rate)
    spread(q3, 0, decay, poles)
    spread(qc3, 0, jnp.exp(-rate * CHUNK), poles)
    spread(qr3, 0, jnp.exp(-rate * rows), poles)
    two = jnp.exp(-2.0 * rate)
    spread(c3, 0, res_ref[...] * jnp.sqrt(jnp.tanh(rate) * (1.0 + two)), poles)
    f3[0:TILE * SUB, :] = jnp.zeros((TILE * SUB, LANES), f32)
    f3[(TILE + taps) * SUB:, :] = jnp.zeros((TILE * SUB, LANES), f32)
    spread(f3, TILE, fir_ref[...], taps)
    y3[...] = jnp.zeros_like(y3)
    inc[...] = jnp.zeros_like(inc)

    def multiply(lhs, origin, first):
        for n in range(0, width, 512):
            cols = slice(n, n + 512)
            block = pl.ds(pl.multiple_of(origin * depth, depth), depth)
            product = jnp.dot(lhs, w_v[block, cols], preferred_element_type=f32)
            if first:
                acc[:, cols] = product
            else:
                acc[:, cols] += product

    def fir_tiles(first, last, low, high):
        def tile(t, carry):
            y = tuple(y3[at_rows(t * TILE + i, 1), :] for i in range(TILE))

            def step(b, y):
                xs = x3[at_rows(taps + 8 * b, 8), :]
                fs = f3[at_rows(TILE + t * TILE - 8 * b - 7, 7 + TILE), :]
                y = list(y)
                for k in range(8):
                    xk = xs[k * SUB:(k + 1) * SUB]
                    for i in range(TILE):
                        m = i - k + 7
                        y[i] = y[i] + fs[m * SUB:(m + 1) * SUB] * xk
                return tuple(y)

            y = lax.fori_loop(jnp.maximum(low, 2 * t - taps // 8),
                              jnp.minimum(high, 2 * t + 2), step, y)
            for i in range(TILE):
                y3[at_rows(t * TILE + i, 1), :] = y[i]
            return carry

        lax.fori_loop(first, last, tile, 0)

    per = CHUNK // TILE
    reach = per + taps // TILE
    tiles = rows // TILE

    def fir_chunk(c, half):
        first = c * per + half * (reach // 2)
        last = jnp.minimum(tiles, first + reach // 2)
        fir_tiles(first, last, c * (CHUNK // 8), (c + 1) * (CHUNK // 8))

    def tree(terms):
        while len(terms) > 1:
            terms = [a + b for a, b in zip(terms[::2], terms[1::2])]
        return terms[0]

    def modal_chunk(c):
        q = [q3[p * SUB:(p + 1) * SUB, :] for p in range(poles)]
        coef = [c3[p * SUB:(p + 1) * SUB, :] for p in range(poles)]

        def step(i, state):
            at = c * CHUNK + i
            x = x3[at_rows(taps + at, 1), :]
            state = tuple(q[p] * state[p] + coef[p] * x for p in range(poles))
            y3[at_rows(at, 1), :] += tree(list(state))
            return state

        zero = jnp.zeros((SUB, LANES), f32)
        state = lax.fori_loop(0, CHUNK, step, (zero,) * poles)
        ends[c] = jnp.concatenate(state, axis=0)

    def tail_copy():
        return pltpu.make_async_remote_copy(
            src_ref=sig.at[pl.ds(rows - taps, taps), :], dst_ref=tail_in,
            send_sem=tail_sem.at[0], recv_sem=tail_sem.at[1],
            device_id={"seq": s + 1}, device_id_type=MESH)

    def fir_tail():
        @pl.when(s > 0)
        def _():
            pltpu.make_async_remote_copy(
                src_ref=tail_in, dst_ref=tail_in,
                send_sem=tail_sem.at[0], recv_sem=tail_sem.at[1],
                device_id={"seq": s - 1}, device_id_type=MESH).wait_recv()
            spread(x3, 0, tail_in[...].astype(f32), taps)
            fir_tiles(0, taps // TILE, -(taps // 8), 0)

    for load in loads[4:]:
        load.wait()
    w_copy(z).wait()

    at_end = (z == 0) | (z == chs - 1)

    def chunk_step(i, carry):
        c = chunks - 1 - i

        @pl.when(i + 1 < chunks)
        def _():
            send_own(c - 1)

        multiply(x_all[z, chunk_rows(c), :], z, True)
        for d in range(1, chs):
            @pl.when((i > 0) & (at_end | (i < chunks - 1)))
            def _():
                if d == 1:
                    modal_chunk(c + 1)
                if d == min(2, chs - 1):
                    fir_chunk(c + 1, 0)
                if d == min(3, chs - 1):
                    fir_chunk(c + 1, 1)

            if d == chs - 1:
                @pl.when((i == chunks - 1) & at_end)
                def _():
                    fir_tail()

            for way in range(2):
                step = 1 - 2 * way

                @pl.when(comes(way, d))
                def _():
                    landed(way, d, c).wait_recv()

                    if d < chs - 1:
                        @pl.when(goes(way))
                        def _():
                            hop(way, d, c).start()

            for way in range(2):
                step = 1 - 2 * way

                @pl.when(comes(way, d))
                def _():
                    origin = z - step * d

                    @pl.when(i == 0)
                    def _():
                        w_copy(origin).wait()
                    multiply(x_all[origin, chunk_rows(c), :], origin, False)

        @pl.when((i == chunks - 1) & jnp.logical_not(at_end))
        def _():
            modal_chunk(c + 1)
            fir_chunk(c + 1, 0)
            fir_chunk(c + 1, 1)
            fir_tail()

        low = (gates_ref[1, chunk_rows(c), :].astype(f32) * acc[...]).astype(bf16)
        sig[chunk_rows(c), :] = low
        spread(x3, taps + c * CHUNK, low.astype(f32), CHUNK)

        @pl.when((i == taps // CHUNK - 1) & (s < seqs - 1))
        def _():
            tail_copy().start()
        return carry

    lax.fori_loop(0, chunks, chunk_step, 0)

    modal_chunk(0)
    total = ends[0]
    for c in range(1, chunks):
        total = qc3[...] * total + ends[c]
    st_out[0] = total

    odd = lax.rem(s, 2)
    pair = s // 2
    pairs_count = seqs // 2
    partner = s + 1 - 2 * odd
    swap = pltpu.make_async_remote_copy(
        src_ref=st_out.at[0], dst_ref=st_mate,
        send_sem=mate_sem.at[0], recv_sem=mate_sem.at[1],
        device_id={"seq": partner}, device_id_type=MESH)
    swap.start()
    fir_chunk(0, 0)
    swap.wait_recv()

    @pl.when(odd == 0)
    def _():
        st_out[1] = qr3[...] * st_out[0] + st_mate[...]

    @pl.when(odd == 1)
    def _():
        st_out[1] = qr3[...] * st_mate[...] + st_out[0]

    def state_copy(other):
        return pltpu.make_async_remote_copy(
            src_ref=st_out.at[1], dst_ref=st_in.at[pair],
            send_sem=st_send_sem.at[other], recv_sem=st_recv_sem.at[pair],
            device_id={"seq": 2 * other + odd}, device_id_type=MESH)

    def start_state(n, carry):
        state_copy(pairs_count + pair - n).start()
        return carry

    lax.fori_loop(pair + 1, pairs_count, start_state, 0)
    fir_chunk(0, 1)

    def take_state(other, carry):
        pltpu.make_async_remote_copy(
            src_ref=st_out.at[1], dst_ref=st_in.at[other],
            send_sem=st_send_sem.at[other], recv_sem=st_recv_sem.at[other],
            device_id={"seq": 2 * other + odd}, device_id_type=MESH).wait_recv()
        inc[...] = qr3[...] * (qr3[...] * inc[...]) + st_in[other]
        return carry

    lax.fori_loop(0, pair, take_state, 0)

    @pl.when(odd == 1)
    def _():
        inc[...] = qr3[...] * inc[...] + st_mate[...]

    def out_copy(c):
        part = slice(c * CHUNK, (c + 1) * CHUNK)
        return pltpu.make_async_copy(out_v.at[part, :], out_ref.at[part, :], out_sem.at[c])

    q = [q3[p * SUB:(p + 1) * SUB, :] for p in range(poles)]
    for c in range(chunks):
        def step(i, state):
            at = c * CHUNK + i
            state = tuple(q[p] * state[p] for p in range(poles))
            y3[at_rows(at, 1), :] += tree(list(state))
            return state

        state = tuple(inc[p * SUB:(p + 1) * SUB, :] for p in range(poles))
        state = lax.fori_loop(0, CHUNK, step, state)
        inc[...] = jnp.concatenate(state, axis=0) + ends[c]
        part = slice(c * CHUNK, (c + 1) * CHUNK)
        for j in range(groups):
            cols = slice(j * LANES, (j + 1) * LANES)
            conv = y3[pl.ds(c * CHUNK * SUB + j, CHUNK, stride=SUB), :]
            direct = skip_ref[:, cols] * sig[part, cols].astype(f32)
            out_v[part, cols] = (gates_ref[0, part, cols].astype(f32) * (conv + direct)).astype(bf16)
        out_copy(c).start()

    def end_state(other, carry):
        state_copy(other).wait_send()
        return carry

    lax.fori_loop(pair + 1, pairs_count, end_state, 0)
    swap.wait_send()

    @pl.when(s < seqs - 1)
    def _():
        tail_copy().wait_send()

    def end_chunk(c, carry):
        for way in range(2):
            for d in range(chs - 1):
                @pl.when(comes(way, d) & goes(way))
                def _():
                    hop(way, d, c).wait_send()
        return carry

    lax.fori_loop(0, chunks, end_chunk, 0)
    for c in range(chunks):
        out_copy(c).wait()


def on_device(inputs, w_value, gates, decay_rate, residue, fir_taps, skip_gain):
    seqs, chs = lax.axis_size("seq"), lax.axis_size("ch")
    rows, depth = inputs.shape
    width = w_value.shape[1]
    taps = fir_taps.shape[0]
    poles = decay_rate.shape[0]
    chunks = rows // CHUNK
    state = (poles * SUB, LANES)
    return pl.pallas_call(
        functools.partial(fused, seqs, chs),
        out_shape=jax.ShapeDtypeStruct((rows, width), bf16),
        in_specs=[pl.BlockSpec(memory_space=pltpu.HBM)] * 7,
        out_specs=pl.BlockSpec(memory_space=pltpu.HBM),
        scratch_shapes=[
            pltpu.VMEM(gates.shape, bf16),
            pltpu.VMEM(decay_rate.shape, f32),
            pltpu.VMEM(residue.shape, f32),
            pltpu.VMEM(fir_taps.shape, f32),
            pltpu.VMEM((1, width), f32),
            pltpu.VMEM((chs, rows, depth), bf16),
            pltpu.VMEM(w_value.shape, bf16),
            pltpu.VMEM((rows, width), bf16),
            pltpu.VMEM(((taps + rows) * SUB, LANES), f32),
            pltpu.VMEM((rows * SUB, LANES), f32),
            pltpu.VMEM(((taps + 2 * TILE) * SUB, LANES), f32),
            pltpu.VMEM(state, f32),
            pltpu.VMEM(state, f32),
            pltpu.VMEM(state, f32),
            pltpu.VMEM(state, f32),
            pltpu.VMEM((chunks,) + state, f32),
            pltpu.VMEM((taps, width), bf16),
            pltpu.VMEM((2,) + state, f32),
            pltpu.VMEM(state, f32),
            pltpu.VMEM((seqs // 2,) + state, f32),
            pltpu.VMEM(state, f32),
            pltpu.VMEM((rows, width), bf16),
            pltpu.VMEM((CHUNK, width), f32),
            pltpu.SemaphoreType.DMA((2, chs, chunks)),
            pltpu.SemaphoreType.DMA((2, chs, chunks)),
            pltpu.SemaphoreType.DMA((chs,)),
            pltpu.SemaphoreType.DMA((6,)),
            pltpu.SemaphoreType.DMA((2,)),
            pltpu.SemaphoreType.DMA((2,)),
            pltpu.SemaphoreType.DMA((seqs // 2,)),
            pltpu.SemaphoreType.DMA((seqs // 2,)),
            pltpu.SemaphoreType.DMA((chunks,)),
        ],
        compiler_params=pltpu.CompilerParams(
            collective_id=0, has_side_effects=True, vmem_limit_bytes=63 * 2**20),
        cost_estimate=pl.CostEstimate(
            flops=2 * rows * depth * chs * width, bytes_accessed=2 * depth * chs * width, transcendentals=0),
    )(inputs, w_value, gates, decay_rate, residue, fir_taps, skip_gain.reshape(1, width))


def solution(mesh):
    in_specs = (
        P("seq", "ch"),
        P(None, "ch"),
        P(None, "seq", "ch"),
        P(None, "ch"),
        P(None, "ch"),
        P(None, "ch"),
        P("ch"),
    )
    out_specs = P("seq", "ch")
    return jax.shard_map(
        on_device, mesh=mesh, in_specs=in_specs, out_specs=out_specs, check_vma=False
    )
```

```python
import functools

import jax
import jax.numpy as jnp
from jax import lax
from jax.experimental import pallas as pl
from jax.experimental.pallas import tpu as pltpu
from jax.sharding import PartitionSpec as P

MESH = pl.DeviceIdType.MESH
SUB = 8
LANES = 128
TILE = 16
CHUNK = 128
f32 = jnp.float32
bf16 = jnp.bfloat16


def fused(seqs, chs, x_ref, w_ref, gates_hbm, rate_hbm, res_hbm, fir_hbm, skip_hbm, out_ref,
          gates_ref, rate_ref, res_ref, fir_ref, skip_ref, x_all, w_v, sig, x3, y3, f3, q3, c3, qc3, qr3, ends, tail_in, st_out, st_mate, st_in, inc, out_v,
          acc, send_sem, recv_sem, w_sem, load_sem, tail_sem, mate_sem, st_send_sem, st_recv_sem, out_sem):
    rows, depth = x_ref.shape
    width = w_ref.shape[1]
    groups = width // LANES
    taps = fir_ref.shape[0]
    poles = rate_ref.shape[0]
    chunks = rows // CHUNK
    state_rows = poles * SUB
    s = lax.axis_index("seq")
    z = lax.axis_index("ch")

    def at_rows(start, size):
        return pl.ds(pl.multiple_of(start * SUB, SUB), size * SUB)

    barrier = pltpu.get_barrier_semaphore()

    def greet(other, carry):
        same = (other - s) * (other - s)
        @pl.when((same > 0) & ((lax.rem(same, 2) == 0) | (same == 1)))
        def _():
            pl.semaphore_signal(barrier, inc=1, device_id={"seq": other}, device_id_type=MESH)
        return carry

    lax.fori_loop(0, seqs, greet, 0)

    @pl.when(z > 0)
    def _():
        pl.semaphore_signal(barrier, inc=1, device_id={"ch": z - 1}, device_id_type=MESH)

    @pl.when(z < chs - 1)
    def _():
        pl.semaphore_signal(barrier, inc=1, device_id={"ch": z + 1}, device_id_type=MESH)

    def w_copy(origin):
        block = pl.ds(pl.multiple_of(origin * depth, depth), depth)
        return pltpu.make_async_copy(w_ref.at[block, :], w_v.at[block, :], w_sem.at[origin])

    pairs = ((rate_hbm, rate_ref), (res_hbm, res_ref), (fir_hbm, fir_ref), (skip_hbm, skip_ref),
             (x_ref, x_all.at[z]), (gates_hbm, gates_ref))
    loads = [pltpu.make_async_copy(src, dst, load_sem.at[n]) for n, (src, dst) in enumerate(pairs)]
    for load in loads:
        load.start()
    w_copy(z).start()
    for d in range(1, chs):
        @pl.when(z - d >= 0)
        def _():
            w_copy(z - d).start()

        @pl.when(z + d <= chs - 1)
        def _():
            w_copy(z + d).start()

    neighbours = jnp.minimum(z, 1) + jnp.minimum(chs - 1 - z, 1)
    beside = jnp.minimum(s, 1) + jnp.minimum(seqs - 1 - s, 1)
    pl.semaphore_wait(barrier, seqs // 2 - 1 + beside + neighbours)

    def chunk_rows(c):
        return pl.ds(pl.multiple_of(c * CHUNK, CHUNK), CHUNK)

    def hop(way, d, c):
        step = 1 - 2 * way
        origin = z - step * d
        src = x_ref.at[chunk_rows(c), :] if d == 0 else x_all.at[origin, chunk_rows(c), :]
        return pltpu.make_async_remote_copy(
            src_ref=src, dst_ref=x_all.at[origin, chunk_rows(c), :],
            send_sem=send_sem.at[way, d, c], recv_sem=recv_sem.at[way, d + 1, c],
            device_id={"ch": z + step}, device_id_type=MESH)

    def landed(way, d, c):
        step = 1 - 2 * way
        origin = z - step * d
        place = x_all.at[origin, chunk_rows(c), :]
        return pltpu.make_async_remote_copy(
            src_ref=place, dst_ref=place,
            send_sem=send_sem.at[way, d, c], recv_sem=recv_sem.at[way, d, c],
            device_id={"ch": z - step}, device_id_type=MESH)

    def comes(way, d):
        return z - d >= 0 if way == 0 else z + d <= chs - 1

    def goes(way):
        return z < chs - 1 if way == 0 else z > 0

    def send_own(c):
        for way in range(2):
            @pl.when(goes(way))
            def _():
                hop(way, 0, c).start()

    send_own(chunks - 1)

    def spread(dst, first, value, count):
        for j in range(groups):
            dst[pl.ds(first * SUB + j, count, stride=SUB), :] = value[:, j * LANES:(j + 1) * LANES]

    for load in loads[:4]:
        load.wait()
    rate = rate_ref[...]
    decay = jnp.exp(-rate)
    spread(q3, 0, decay, poles)
    spread(qc3, 0, jnp.exp(-rate * CHUNK), poles)
    spread(qr3, 0, jnp.exp(-rate * rows), poles)
    two = jnp.exp(-2.0 * rate)
    spread(c3, 0, res_ref[...] * jnp.sqrt(jnp.tanh(rate) * (1.0 + two)), poles)
    f3[0:TILE * SUB, :] = jnp.zeros((TILE * SUB, LANES), f32)
    f3[(TILE + taps) * SUB:, :] = jnp.zeros((TILE * SUB, LANES), f32)
    spread(f3, TILE, fir_ref[...], taps)
    y3[...] = jnp.zeros_like(y3)
    inc[...] = jnp.zeros_like(inc)

    def multiply(lhs, origin, first):
        for n in range(0, width, 512):
            cols = slice(n, n + 512)
            block = pl.ds(pl.multiple_of(origin * depth, depth), depth)
            product = jnp.dot(lhs, w_v[block, cols], preferred_element_type=f32)
            if first:
                acc[:, cols] = product
            else:
                acc[:, cols] += product

    def fir_tiles(first, last, low, high):
        def tile(t, carry):
            y = tuple(y3[at_rows(t * TILE + i, 1), :] for i in range(TILE))

            def step(b, y):
                xs = x3[at_rows(taps + 8 * b, 8), :]
                fs = f3[at_rows(TILE + t * TILE - 8 * b - 7, 7 + TILE), :]
                y = list(y)
                for k in range(8):
                    xk = xs[k * SUB:(k + 1) * SUB]
                    for i in range(TILE):
                        m = i - k + 7
                        y[i] = y[i] + fs[m * SUB:(m + 1) * SUB] * xk
                return tuple(y)

            y = lax.fori_loop(jnp.maximum(low, 2 * t - taps // 8),
                              jnp.minimum(high, 2 * t + 2), step, y)
            for i in range(TILE):
                y3[at_rows(t * TILE + i, 1), :] = y[i]
            return carry

        lax.fori_loop(first, last, tile, 0)

    per = CHUNK // TILE
    reach = per + taps // TILE
    tiles = rows // TILE

    def fir_chunk(c, half):
        first = c * per + half * (reach // 2)
        last = jnp.minimum(tiles, first + reach // 2)
        fir_tiles(first, last, c * (CHUNK // 8), (c + 1) * (CHUNK // 8))

    def tree(terms):
        while len(terms) > 1:
            terms = [a + b for a, b in zip(terms[::2], terms[1::2])]
        return terms[0]

    def modal_chunk(c):
        q = [q3[p * SUB:(p + 1) * SUB, :] for p in range(poles)]
        coef = [c3[p * SUB:(p + 1) * SUB, :] for p in range(poles)]

        def step(i, state):
            at = c * CHUNK + i
            x = x3[at_rows(taps + at, 1), :]
            state = tuple(q[p] * state[p] + coef[p] * x for p in range(poles))
            y3[at_rows(at, 1), :] += tree(list(state))
            return state

        zero = jnp.zeros((SUB, LANES), f32)
        state = lax.fori_loop(0, CHUNK, step, (zero,) * poles)
        ends[c] = jnp.concatenate(state, axis=0)

    def tail_copy():
        return pltpu.make_async_remote_copy(
            src_ref=sig.at[pl.ds(rows - taps, taps), :], dst_ref=tail_in,
            send_sem=tail_sem.at[0], recv_sem=tail_sem.at[1],
            device_id={"seq": s + 1}, device_id_type=MESH)

    def fir_tail():
        @pl.when(s > 0)
        def _():
            pltpu.make_async_remote_copy(
                src_ref=tail_in, dst_ref=tail_in,
                send_sem=tail_sem.at[0], recv_sem=tail_sem.at[1],
                device_id={"seq": s - 1}, device_id_type=MESH).wait_recv()
            spread(x3, 0, tail_in[...].astype(f32), taps)
            fir_tiles(0, taps // TILE, -(taps // 8), 0)

    for load in loads[4:]:
        load.wait()
    w_copy(z).wait()

    at_end = (z == 0) | (z == chs - 1)

    def chunk_step(i, carry):
        c = chunks - 1 - i

        @pl.when(i + 1 < chunks)
        def _():
            send_own(c - 1)

        multiply(x_all[z, chunk_rows(c), :], z, True)
        for d in range(1, chs):
            @pl.when((i > 0) & (at_end | (i < chunks - 1)))
            def _():
                if d == 1:
                    modal_chunk(c + 1)
                if d == min(2, chs - 1):
                    fir_chunk(c + 1, 0)
                if d == min(3, chs - 1):
                    fir_chunk(c + 1, 1)

            if d == chs - 1:
                @pl.when((i == chunks - 1) & at_end)
                def _():
                    fir_tail()

            for way in range(2):
                step = 1 - 2 * way

                @pl.when(comes(way, d))
                def _():
                    landed(way, d, c).wait_recv()

                    if d < chs - 1:
                        @pl.when(goes(way))
                        def _():
                            hop(way, d, c).start()

            for way in range(2):
                step = 1 - 2 * way

                @pl.when(comes(way, d))
                def _():
                    origin = z - step * d

                    @pl.when(i == 0)
                    def _():
                        w_copy(origin).wait()
                    multiply(x_all[origin, chunk_rows(c), :], origin, False)

        @pl.when((i == chunks - 1) & jnp.logical_not(at_end))
        def _():
            modal_chunk(c + 1)
            fir_chunk(c + 1, 0)
            fir_chunk(c + 1, 1)
            fir_tail()

        low = (gates_ref[1, chunk_rows(c), :].astype(f32) * acc[...]).astype(bf16)
        sig[chunk_rows(c), :] = low
        spread(x3, taps + c * CHUNK, low.astype(f32), CHUNK)

        @pl.when((i == taps // CHUNK - 1) & (s < seqs - 1))
        def _():
            tail_copy().start()
        return carry

    lax.fori_loop(0, chunks, chunk_step, 0)

    modal_chunk(0)
    total = ends[0]
    for c in range(1, chunks):
        total = qc3[...] * total + ends[c]
    st_out[0] = total

    odd = lax.rem(s, 2)
    pair = s // 2
    pairs_count = seqs // 2
    partner = s + 1 - 2 * odd
    swap = pltpu.make_async_remote_copy(
        src_ref=st_out.at[0], dst_ref=st_mate,
        send_sem=mate_sem.at[0], recv_sem=mate_sem.at[1],
        device_id={"seq": partner}, device_id_type=MESH)
    swap.start()
    fir_chunk(0, 0)
    swap.wait_recv()

    @pl.when(odd == 0)
    def _():
        st_out[1] = qr3[...] * st_out[0] + st_mate[...]

    @pl.when(odd == 1)
    def _():
        st_out[1] = qr3[...] * st_mate[...] + st_out[0]

    def state_copy(other):
        return pltpu.make_async_remote_copy(
            src_ref=st_out.at[1], dst_ref=st_in.at[pair],
            send_sem=st_send_sem.at[other], recv_sem=st_recv_sem.at[pair],
            device_id={"seq": 2 * other + odd}, device_id_type=MESH)

    def start_state(n, carry):
        state_copy(pairs_count + pair - n).start()
        return carry

    lax.fori_loop(pair + 1, pairs_count, start_state, 0)
    fir_chunk(0, 1)

    def take_state(other, carry):
        pltpu.make_async_remote_copy(
            src_ref=st_out.at[1], dst_ref=st_in.at[other],
            send_sem=st_send_sem.at[other], recv_sem=st_recv_sem.at[other],
            device_id={"seq": 2 * other + odd}, device_id_type=MESH).wait_recv()
        inc[...] = qr3[...] * (qr3[...] * inc[...]) + st_in[other]
        return carry

    lax.fori_loop(0, pair, take_state, 0)

    @pl.when(odd == 1)
    def _():
        inc[...] = qr3[...] * inc[...] + st_mate[...]

    def out_copy(c):
        part = slice(c * CHUNK, (c + 1) * CHUNK)
        return pltpu.make_async_copy(out_v.at[part, :], out_ref.at[part, :], out_sem.at[c])

    q = [q3[p * SUB:(p + 1) * SUB, :] for p in range(poles)]
    for c in range(chunks):
        def step(i, state):
            at = c * CHUNK + i
            state = tuple(q[p] * state[p] for p in range(poles))
            y3[at_rows(at, 1), :] += tree(list(state))
            return state

        state = tuple(inc[p * SUB:(p + 1) * SUB, :] for p in range(poles))
        state = lax.fori_loop(0, CHUNK, step, state)
        inc[...] = jnp.concatenate(state, axis=0) + ends[c]
        part = slice(c * CHUNK, (c + 1) * CHUNK)
        for j in range(groups):
            cols = slice(j * LANES, (j + 1) * LANES)
            conv = y3[pl.ds(c * CHUNK * SUB + j, CHUNK, stride=SUB), :]
            direct = skip_ref[:, cols] * sig[part, cols].astype(f32)
            out_v[part, cols] = (gates_ref[0, part, cols].astype(f32) * (conv + direct)).astype(bf16)
        out_copy(c).start()

    def end_state(other, carry):
        state_copy(other).wait_send()
        return carry

    lax.fori_loop(pair + 1, pairs_count, end_state, 0)
    swap.wait_send()

    @pl.when(s < seqs - 1)
    def _():
        tail_copy().wait_send()

    def end_chunk(c, carry):
        for way in range(2):
            for d in range(chs - 1):
                @pl.when(comes(way, d) & goes(way))
                def _():
                    hop(way, d, c).wait_send()
        return carry

    lax.fori_loop(0, chunks, end_chunk, 0)
    for c in range(chunks):
        out_copy(c).wait()


def on_device(inputs, w_value, gates, decay_rate, residue, fir_taps, skip_gain):
    seqs, chs = lax.axis_size("seq"), lax.axis_size("ch")
    rows, depth = inputs.shape
    width = w_value.shape[1]
    taps = fir_taps.shape[0]
    poles = decay_rate.shape[0]
    chunks = rows // CHUNK
    state = (poles * SUB, LANES)
    return pl.pallas_call(
        functools.partial(fused, seqs, chs),
        out_shape=jax.ShapeDtypeStruct((rows, width), bf16),
        in_specs=[pl.BlockSpec(memory_space=pltpu.HBM)] * 7,
        out_specs=pl.BlockSpec(memory_space=pltpu.HBM),
        scratch_shapes=[
            pltpu.VMEM(gates.shape, bf16),
            pltpu.VMEM(decay_rate.shape, f32),
            pltpu.VMEM(residue.shape, f32),
            pltpu.VMEM(fir_taps.shape, f32),
            pltpu.VMEM((1, width), f32),
            pltpu.VMEM((chs, rows, depth), bf16),
            pltpu.VMEM(w_value.shape, bf16),
            pltpu.VMEM((rows, width), bf16),
            pltpu.VMEM(((taps + rows) * SUB, LANES), f32),
            pltpu.VMEM((rows * SUB, LANES), f32),
            pltpu.VMEM(((taps + 2 * TILE) * SUB, LANES), f32),
            pltpu.VMEM(state, f32),
            pltpu.VMEM(state, f32),
            pltpu.VMEM(state, f32),
            pltpu.VMEM(state, f32),
            pltpu.VMEM((chunks,) + state, f32),
            pltpu.VMEM((taps, width), bf16),
            pltpu.VMEM((2,) + state, f32),
            pltpu.VMEM(state, f32),
            pltpu.VMEM((seqs // 2,) + state, f32),
            pltpu.VMEM(state, f32),
            pltpu.VMEM((rows, width), bf16),
            pltpu.VMEM((CHUNK, width), f32),
            pltpu.SemaphoreType.DMA((2, chs, chunks)),
            pltpu.SemaphoreType.DMA((2, chs, chunks)),
            pltpu.SemaphoreType.DMA((chs,)),
            pltpu.SemaphoreType.DMA((6,)),
            pltpu.SemaphoreType.DMA((2,)),
            pltpu.SemaphoreType.DMA((2,)),
            pltpu.SemaphoreType.DMA((seqs // 2,)),
            pltpu.SemaphoreType.DMA((seqs // 2,)),
            pltpu.SemaphoreType.DMA((chunks,)),
        ],
        compiler_params=pltpu.CompilerParams(
            collective_id=0, has_side_effects=True, vmem_limit_bytes=63 * 2**20),
        cost_estimate=pl.CostEstimate(
            flops=2 * rows * depth * chs * width, bytes_accessed=2 * depth * chs * width, transcendentals=0),
    )(inputs, w_value, gates, decay_rate, residue, fir_taps, skip_gain.reshape(1, width))


def solution(mesh):
    in_specs = (
        P("seq", "ch"),
        P(None, "ch"),
        P(None, "seq", "ch"),
        P(None, "ch"),
        P(None, "ch"),
        P(None, "ch"),
        P("ch"),
    )
    out_specs = P("seq", "ch")
    return jax.shard_map(
        on_device, mesh=mesh, in_specs=in_specs, out_specs=out_specs, check_vma=False
    )
```
